32 devices in a mesh: dp: 8 (over z, y), comp: 4 (over x, core).
Axes of the slice: x: 2, y: 2, z: 4, core: 2. Of those that a mesh axis runs over, the one named last changes fastest.
Arguments:
- points: bfloat16 [4096, 1024], P('dp'), may hold values from -6 to 6
- means: float32 [1024, 8192], P('dp', 'comp'), may hold values from -2.25 to 2.25
- variances: float32 [1024, 8192], P('dp', 'comp'), may hold values from 0.45 to 2.22
- log_weights: float32 [8192], P('comp'), may hold values from -4 to 4
- split_list: int32 [256, 2], replicated, may hold values from 0 to 8191, as said below
- prune_list: int32 [256], replicated, may hold values from 0 to 8191, as said below
Outputs:
- new_means: float32 [1024, 8192], P('dp', 'comp')
- new_variances: float32 [1024, 8192], P('dp', 'comp')
- new_log_weights: float32 [8192], P('comp')
The draws below stay inside these ranges and needn't reach their ends.
Inputs may be any that keep to these rules, and one draw needn't show every extreme that they name: `split_list`: rows j * 64 to (j + 1) * 64 - 1 of column 0 name 64 distinct components among j * 2048 to (j + 1) * 2048 - 1; column 1 is a permutation of 0 to 255. `prune_list`: distinct components, none of them in column 0 of split_list, exactly 64 in each aligned block of 2048 ids.
All inputs are finite; a program needn't handle non-finite values.
Results may differ from the reference program's by a relative error of at most 0.004.
The reference program's roundings to bfloat16 on the way (of `x_sq` and `resp`) count: a program that leaves them out, or rounds other values in their place, can miss the bound.
Values may be sent and summed in bfloat16 or wider, within the bound.
A program may use at most 64 MiB of HBM per device.

```python
import math
import jax
import jax.numpy as jnp
from jax import lax

D = 1024
K_DEV = 2048
SPL_DEV = 64
COMPONENTS = 8192
NPTS = 4096
SPLITS = 256


def split_plan(key):
    base_key = jax.random.fold_in(key, 4242)
    blocks = COMPONENTS // K_DEV
    block_keys = jax.random.split(jax.random.fold_in(base_key, 1), blocks)
    orders = jax.vmap(lambda one_key: jax.random.permutation(one_key, K_DEV))(block_keys).astype(jnp.int32)
    orders = orders + (jnp.arange(blocks, dtype=jnp.int32) * K_DEV)[:, None]
    sources = orders[:, :SPL_DEV].reshape(-1)
    pruned = orders[:, SPL_DEV:2 * SPL_DEV].reshape(-1)
    shuffle = jax.random.permutation(jax.random.fold_in(base_key, 2), SPLITS).astype(jnp.int32)
    prune_order = pruned[shuffle]
    slot_index = jax.random.permutation(jax.random.fold_in(base_key, 3), SPLITS).astype(jnp.int32)
    return (jnp.stack([sources, slot_index], 1).astype(jnp.int32), prune_order.astype(jnp.int32))


def draw_split_list(key, part):
    return split_plan(key)[0]


def draw_prune_list(key, part):
    return split_plan(key)[1]


def perturbation(noise_key):
    noise = jnp.clip(jax.random.normal(noise_key, (D, COMPONENTS), jnp.float32), -5.0, 5.0)
    return noise


def draw_means(key, part):
    base_key = jax.random.fold_in(key, 7101)
    profile = jnp.clip(0.5 * jax.random.normal(jax.random.fold_in(base_key, 1), (D,), jnp.float32), -2.0, 2.0)
    noise = perturbation(jax.random.fold_in(base_key, 2))
    return profile[:, None] + 0.05 * noise


def draw_variances(key, part):
    base_key = jax.random.fold_in(key, 7202)
    low = math.log(0.5)
    high = math.log(2.0)
    profile = jax.random.uniform(jax.random.fold_in(base_key, 1), (D,), jnp.float32, low, high)
    noise = perturbation(jax.random.fold_in(base_key, 2))
    return jnp.exp(profile[:, None] + 0.02 * noise)


def levels(key, extent, cuts, least, largest):
    factor_of, own = 1.0, jax.random.fold_in(key, 6)
    for axis_at, blocks in cuts:
        steps = jnp.exp(jax.random.uniform(jax.random.fold_in(own, axis_at), (blocks,), jnp.float32, least / len(cuts), largest / len(cuts)))
        factor_of = factor_of * jnp.repeat(steps, extent[axis_at] // blocks).reshape([-1 if axis == axis_at else 1 for axis in range(len(extent))])
    return factor_of


def centred(stream_key, dims, width, most, pieces=(), kind=jnp.bfloat16):
    gain = levels(stream_key, dims, pieces, -0.22, 0.18) if pieces else 1.0
    drawn = jax.random.normal(stream_key, dims, jnp.float32) * width * gain
    return jnp.minimum(jnp.maximum(drawn, -most), most).astype(kind)


def setup_inputs(seed: int = 0) -> dict:
    arg_keys = jax.random.split(jax.random.key(seed), 7)
    points = centred(arg_keys[0], (NPTS, D), 1.0, 6.0, ((0, 8),))
    means = draw_means(jax.random.fold_in(arg_keys[6], 71), 0)
    variances = draw_variances(jax.random.fold_in(arg_keys[6], 71), 0)
    log_weights = centred(arg_keys[3], (COMPONENTS,), 1.0, 4.0, ((0, 4),), jnp.float32)
    split_list = draw_split_list(jax.random.fold_in(arg_keys[6], 71), 0)
    prune_list = draw_prune_list(jax.random.fold_in(arg_keys[6], 71), 0)
    return dict(points=points, means=means, variances=variances, log_weights=log_weights, split_list=split_list, prune_list=prune_list)


log_two_pi = math.log(2.0 * math.pi)
log_two = math.log(2.0)
prior_count = 1.0
split_scale = 0.5

def block_scores(points, x_sq, means_block, vars_block, weights_block):
    precision = 1.0 / vars_block
    prec_low = precision.astype(jnp.bfloat16)
    pm_low = (precision * means_block).astype(jnp.bfloat16)
    const = weights_block + 0.5 * lax.optimization_barrier(jnp.sum(jnp.log(precision), 0)) - 0.5 * lax.optimization_barrier(jnp.sum(precision * means_block * means_block, 0)) - 0.5 * D * log_two_pi
    quad = jnp.dot(x_sq, prec_low, preferred_element_type=jnp.float32)
    lin = jnp.dot(points, pm_low, preferred_element_type=jnp.float32)
    return -0.5 * quad + lin + const[None, :]

def reference(points, means, variances, log_weights, split_list, prune_list):
    blocks = COMPONENTS // K_DEV
    mean_blocks = means.reshape(D, blocks, K_DEV).transpose(1, 0, 2)
    var_blocks = variances.reshape(D, blocks, K_DEV).transpose(1, 0, 2)
    weight_blocks = log_weights.reshape(blocks, K_DEV)
    as_float = points.astype(jnp.float32)
    x_sq = (as_float * as_float).astype(jnp.bfloat16)

    def first_pass(operands):
        scores = block_scores(points, x_sq, operands[0], operands[1], operands[2])
        top = lax.optimization_barrier(jnp.max(scores, 1))
        return (top, lax.optimization_barrier(jnp.sum(jnp.exp(scores - top[:, None]), 1)))
    maxes, totals = lax.map(first_pass, (mean_blocks, var_blocks, weight_blocks))
    highest = lax.optimization_barrier(jnp.max(maxes, 0))
    lse = highest + jnp.log(lax.optimization_barrier(jnp.sum(totals * jnp.exp(maxes - highest[None, :]), 0)))
    contract = (((0,), (0,)), ((), ()))

    def second_pass(operands):
        scores = block_scores(points, x_sq, operands[0], operands[1], operands[2])
        resp = jnp.exp(scores - lse[:, None]).astype(jnp.bfloat16)
        counts = lax.optimization_barrier(jnp.sum(resp, 0, dtype=jnp.float32))
        sum_x = lax.dot_general(points, resp, contract, preferred_element_type=jnp.float32)
        sum_xx = lax.dot_general(x_sq, resp, contract, preferred_element_type=jnp.float32)
        return (counts, sum_x, sum_xx)
    counts, sum_x, sum_xx = lax.map(second_pass, (mean_blocks, var_blocks, weight_blocks))
    counts = counts.reshape(COMPONENTS)
    sum_x = sum_x.transpose(1, 0, 2).reshape(D, COMPONENTS)
    sum_xx = sum_xx.transpose(1, 0, 2).reshape(D, COMPONENTS)
    total = counts + prior_count
    mean_new = (sum_x + prior_count * means) / total[None, :]
    var_new = (sum_xx + prior_count * (variances + means * means)) / total[None, :] - mean_new * mean_new
    lw_new = jnp.log(total) - jnp.log(NPTS + COMPONENTS * prior_count)
    sources = split_list[:, 0]
    targets = prune_list[split_list[:, 1]]
    src_mean = mean_new[:, sources]
    src_var = var_new[:, sources]
    shift = split_scale * jnp.sqrt(src_var)
    new_means = mean_new.at[:, sources].add(shift)
    new_means = new_means.at[:, targets].set(src_mean - shift)
    new_variances = var_new.at[:, targets].set(src_var)
    src_weight = lw_new[sources] - log_two
    new_log_weights = lw_new.at[sources].set(src_weight)
    new_log_weights = new_log_weights.at[targets].set(src_weight)
    return (new_means, new_variances, new_log_weights)
```

```python
import functools
import math

import jax
import jax.numpy as jnp
from jax import lax
from jax.experimental import pallas as pl
from jax.experimental.pallas import tpu as pltpu
from jax.sharding import PartitionSpec as P

log_two_pi = math.log(2.0 * math.pi)
log_two = math.log(2.0)
prior_count = 1.0
split_scale = 0.5
MESH = pl.DeviceIdType.MESH
BF = jnp.bfloat16
F32 = jnp.float32
NT = (((1,), (1,)), ((), ()))


def aligned(index, step):
    return pl.ds(pl.multiple_of(index * step, step), step)


def kernel(
    n_dp, n_comp,
    pts, means, variances, weights, split, prune,
    out_mean, out_var, out_weight,
    allp, prm, par, par_t, cst_s, cst_r, scores, part_c, part_d, lse, resp,
    mom_s, mom_r, cnt_s, cnt_r, new_m, new_v, new_w, pay, got,
    z_s, z_r, y_s, y_r, x_s, x_r, c_s, c_r, p_s, p_r, k_s, k_r,
    lc_s, lc_r, ld_s, ld_r, m_s, m_r, n_s, n_r, g_s, g_r,
):
    rows, feats = pts.shape
    width, k_dev = means.shape
    chunk = k_dev // n_dp
    piece = rows // n_comp
    spl = split.shape[0] // n_comp
    far = 4 if n_dp % 4 == 0 else 1
    near = n_dp // far
    pairs = n_comp // 2
    i = lax.axis_index("dp")
    j = lax.axis_index("comp")
    a, b = i // near, i % near
    pair, core = j // 2, j % 2

    barrier = pltpu.get_barrier_semaphore()
    for r in range(1, n_dp):
        pl.semaphore_signal(barrier, inc=1, device_id=((i + r) % n_dp, j), device_id_type=MESH)
    for r in range(1, n_comp):
        pl.semaphore_signal(barrier, inc=1, device_id=(i, (j + r) % n_comp), device_id_type=MESH)
    pl.semaphore_wait(barrier, n_dp + n_comp - 2)

    def remote(src, dst, send, recv, to_i, to_j):
        return pltpu.make_async_remote_copy(
            src_ref=src, dst_ref=dst, send_sem=send, recv_sem=recv,
            device_id=(to_i, to_j), device_id_type=MESH,
        )

    def block_of(s, t):
        return ((a + far - s) % far) * near + (b + near - t) % near

    def place(block, quarter):
        return allp.at[aligned(block * n_comp + quarter, piece), :]

    def own_piece():
        return pts.at[aligned(j, piece), :]

    def z_copy(s):
        return remote(own_piece(), place(i, j), z_s.at[s], z_r.at[s], ((a + s) % far) * near + b, j)

    def y_copy(s, t):
        src = place(block_of(s, 0), j)
        return remote(src, src, y_s.at[s, t], y_r.at[s, t], a * near + (b + t) % near, j)

    def x_copy(idx, u):
        src = place(block_of(idx // near, idx % near), j)
        return remote(src, src, x_s.at[idx, u], x_r.at[idx, u], i, ((pair + u) % pairs) * 2 + core)

    def c_copy(idx, u):
        quarter = ((pair + pairs - u) % pairs) * 2 + core
        src = place(block_of(idx // near, idx % near), quarter)
        return remote(src, src, c_s.at[idx, u], c_r.at[idx, u], i, pair * 2 + 1 - core)

    for s in range(1, far):
        z_copy(s).start()
    allp[aligned(i, rows), :] = pts[...]
    for t in range(1, near):
        y_copy(0, t).start()

    def make_params(to):
        cols = aligned(to, chunk)
        v = variances[:, cols]
        m = means[:, cols]
        p = 1.0 / v
        pm = p * m
        prm[0, :, cols] = p.astype(BF)
        prm[1, :, cols] = pm.astype(BF)
        part = -0.5 * jnp.sum(jnp.log(v) + pm * m, 0, keepdims=True)
        cst_s[:, cols] = jnp.broadcast_to(part, (8, chunk))

    def p_copy(r):
        to = (i + r) % n_dp
        return remote(prm.at[:, :, aligned(to, chunk)], par.at[:, aligned(i, width), :], p_s.at[r], p_r.at[r], to, j)

    def k_copy(r):
        to = (i + r) % n_dp
        return remote(cst_s.at[:, aligned(to, chunk)], cst_r.at[i], k_s.at[r], k_r.at[r], to, j)

    def send_params(r, carry):
        make_params((i + r) % n_dp)
        p_copy(r).start()
        k_copy(r).start()
        return carry

    lax.fori_loop(1, n_dp, send_params, 0)
    make_params(i)
    par[:, aligned(i, width), :] = prm[:, :, aligned(i, chunk)]
    cst_r[i] = cst_s[:, aligned(i, chunk)]

    def pass_on(idx):
        for u in range(1, pairs):
            x_copy(idx, u).start()
        c_copy(idx, 0).start()

    for s in range(1, far):
        z_copy(s).wait_recv()
        for t in range(1, near):
            y_copy(s, t).start()
        pass_on(s * near)
    for s in range(far):
        for t in range(1, near):
            y_copy(s, t).wait_recv()
            pass_on(s * near + t)

    def wait_params(r, carry):
        p_copy(r).wait_recv()
        k_copy(r).wait_recv()
        return carry

    lax.fori_loop(1, n_dp, wait_params, 0)
    par_t[0] = (-0.5 * par[0].astype(F32)).T.astype(BF)
    par_t[1] = par[1].astype(F32).T.astype(BF)
    const_row = jnp.sum(cst_r[...], 0) + weights[:, aligned(i, chunk)] - 0.5 * feats * log_two_pi
    const = const_row.T[:, :1]

    def score(block):
        x = allp[aligned(block, rows), :]
        s = (
            lax.dot_general(par_t[0], x * x, NT, preferred_element_type=F32)
            + lax.dot_general(par_t[1], x, NT, preferred_element_type=F32)
            + const
        )
        scores[block] = s
        top = jnp.max(s, 0, keepdims=True)
        part_c[j, pl.ds(block, 1), :] = top + jnp.log(jnp.sum(jnp.exp(s - top), 0, keepdims=True))

    score(i)

    def score_step(idx, carry):
        for u in range(1, pairs):
            x_copy(idx, u).wait_recv()
            c_copy(idx, u).start()
        for u in range(pairs):
            c_copy(idx, u).wait_recv()
        score(block_of(idx // near, idx % near))
        return carry

    lax.fori_loop(1, n_dp, score_step, 0)

    def joined(parts):
        top = jnp.max(parts, 0)
        return top + jnp.log(jnp.sum(jnp.exp(parts - top[None]), 0))

    def lc_copy(r):
        return remote(part_c.at[j], part_c.at[j], lc_s.at[r], lc_r.at[r], i, (j + r) % n_comp)

    def ld_copy(r):
        return remote(part_d.at[i], part_d.at[i], ld_s.at[r], ld_r.at[r], (i + r) % n_dp, j)

    for r in range(1, n_comp):
        lc_copy(r).start()
    for r in range(1, n_comp):
        lc_copy(r).wait_recv()
    part_d[i] = joined(part_c[...])
    for r in range(1, n_dp):
        ld_copy(r).start()
    for r in range(1, n_dp):
        ld_copy(r).wait_recv()
    lse[...] = joined(part_d[...])

    def respond(block, carry):
        value = jnp.exp(scores[block] - lse[pl.ds(block, 1), :]).astype(BF)
        resp[:, aligned(block, rows)] = value
        return carry + lax.dot_general(jnp.ones((8, rows), BF), value, NT, preferred_element_type=F32)

    cnt_s[...] = lax.fori_loop(0, n_dp, respond, jnp.zeros((8, chunk), F32))

    def n_copy(r):
        return remote(cnt_s, cnt_r.at[:, aligned(i, chunk)], n_s.at[r], n_r.at[r], (i + r) % n_dp, j)

    for r in range(1, n_dp):
        n_copy(r).start()
    cnt_r[:, aligned(i, chunk)] = cnt_s[...]

    def m_copy(r):
        to = (i + r) % n_dp
        return remote(
            mom_s.at[:, aligned(to, width), :], mom_r.at[:, :, aligned(i, chunk)], m_s.at[r], m_r.at[r], to, j
        )

    wide = max(width, 256)
    each = wide // width
    groups = feats // wide
    mine = i // each

    def moment(group):
        cols = aligned(group, wide)
        x = allp[:, cols]
        mom_s[0, cols, :] = jnp.dot(resp[...], x, preferred_element_type=F32).T.astype(BF)
        mom_s[1, cols, :] = jnp.dot(resp[...], x * x, preferred_element_type=F32).T.astype(BF)

    def moment_step(g, carry):
        group = (mine + g) % groups
        moment(group)
        for e in range(each):
            m_copy((group * each + e + n_dp - i) % n_dp).start()
        return carry

    lax.fori_loop(1, groups, moment_step, 0)
    moment(mine)
    for e in range(1, each):
        to = mine * each + (i % each + e) % each
        m_copy((to + n_dp - i) % n_dp).start()
    mom_r[:, :, aligned(i, chunk)] = mom_s[:, aligned(i, width), :]

    base = (j * k_dev).astype(F32)
    sources = split[aligned(j, spl), :][:, 0:1].astype(F32) - base
    n_total = math.log(n_dp * rows + n_comp * k_dev * prior_count)
    pay[...] = jnp.zeros_like(pay)

    def hot(ids, at):
        ids_at = lax.broadcasted_iota(jnp.int32, (ids.shape[0], chunk), 1) + at * chunk
        return ids == ids_at.astype(F32)

    def finish(at):
        cols = aligned(at, chunk)
        total = cnt_r[0:1, cols] + prior_count
        inverse = 1.0 / total
        old = means[:, cols]
        mean = (mom_r[0, :, cols].astype(F32) + prior_count * old) * inverse
        var = (mom_r[1, :, cols].astype(F32) + prior_count * (variances[:, cols] + old * old)) * inverse - mean * mean
        low = jnp.log(total) - n_total
        here = hot(sources, at)
        here_f = jnp.where(here, 1.0, 0.0)
        source = jnp.max(here_f, 0, keepdims=True)
        shift = jnp.where(source > 0.5, split_scale * jnp.sqrt(var), 0.0)
        low = low - log_two * source
        new_m[:, cols] = mean + shift
        new_v[:, cols] = var
        new_w[:, cols] = low
        low_high = low.astype(BF)
        low_rest = (low - low_high.astype(F32)).astype(BF)
        here_b = here_f.astype(BF)
        pay[0, :width, :] += lax.dot_general((mean - shift).astype(BF), here_b, NT, preferred_element_type=F32)
        pay[1, :width, :] += lax.dot_general(var.astype(BF), here_b, NT, preferred_element_type=F32)
        spread = lambda row: jnp.broadcast_to(row, (8, chunk))
        pay[0, width:, :] += lax.dot_general(spread(low_high), here_b, NT, preferred_element_type=F32)
        pay[1, width:, :] += lax.dot_general(spread(low_rest), here_b, NT, preferred_element_type=F32)

    finish(i)

    def finish_step(r, carry):
        n_copy(r).wait_recv()
        m_copy(r).wait_recv()
        finish((i + n_dp - r) % n_dp)
        return carry

    lax.fori_loop(1, n_dp, finish_step, 0)

    extra = 16
    got[j, :width, :] = jnp.concatenate([pay[0, :width, :], pay[1, :width, :]], 1).astype(BF)
    got[j, width : width + extra, :] = jnp.concatenate(
        [
            jnp.concatenate([pay[0, width:, :], pay[1, width:, :]], 1),
            jnp.ones((8, 2 * spl), F32),
        ],
        0,
    ).astype(BF)

    def g_copy(r):
        return remote(got.at[j], got.at[j], g_s.at[r], g_r.at[r], i, (j + r) % n_comp)

    for r in range(1, n_comp):
        g_copy(r).start()
    slots = split[:, 1:2]
    slot_at = lax.broadcasted_iota(jnp.int32, (split.shape[0], split.shape[0]), 1)
    targets = jnp.sum(jnp.where(slots == slot_at, prune[...].astype(F32), 0.0), 1, keepdims=True) - base
    blank = jnp.full((spl, 1), -1.0, F32)
    parts = [targets[q * spl : (q + 1) * spl] for q in range(n_comp)]
    left = jnp.concatenate([part for q in range(n_comp) for part in (parts[q], blank)], 0)
    right = jnp.concatenate([part for q in range(n_comp) for part in (blank, parts[q])], 0)
    for r in range(1, n_comp):
        g_copy(r).wait_recv()
    cat = jnp.concatenate([got[q] for q in range(n_comp)], 1)

    for at in range(n_dp):
        cols = pl.ds(at * chunk, chunk)
        hot_l = jnp.where(hot(left, at), 1.0, 0.0).astype(BF)
        hot_r = jnp.where(hot(right, at), 1.0, 0.0).astype(BF)
        got_m = jnp.dot(cat, hot_l, preferred_element_type=F32)
        got_v = jnp.dot(cat, hot_r, preferred_element_type=F32)
        takes = got_m[width + 8 : width + 9, :] > 0.5
        out_mean[:, cols] = jnp.where(takes, got_m[:width], new_m[:, cols])
        out_var[:, cols] = jnp.where(takes, got_v[:width], new_v[:, cols])
        moved = got_m[width : width + 1, :] + got_v[width : width + 1, :]
        out_weight[:, cols] = jnp.where(takes, moved, new_w[:, cols])

    for s in range(1, far):
        z_copy(s).wait_send()
    for s in range(far):
        for t in range(1, near):
            y_copy(s, t).wait_send()

    def drain(idx, carry):
        for u in range(1, pairs):
            x_copy(idx, u).wait_send()
        for u in range(pairs):
            c_copy(idx, u).wait_send()
        p_copy(idx).wait_send()
        k_copy(idx).wait_send()
        ld_copy(idx).wait_send()
        n_copy(idx).wait_send()
        m_copy(idx).wait_send()
        return carry

    lax.fori_loop(1, n_dp, drain, 0)
    for r in range(1, n_comp):
        lc_copy(r).wait_send()
        g_copy(r).wait_send()


def solution(mesh):
    n_dp, n_comp = mesh.shape["dp"], mesh.shape["comp"]

    def per_device(points, means, variances, log_weights, split_list, prune_list):
        rows, feats = points.shape
        width, k_dev = means.shape
        chunk = k_dev // n_dp
        npts = rows * n_dp
        spl = split_list.shape[0] // n_comp
        far = 4 if n_dp % 4 == 0 else 1
        near, pairs = n_dp // far, n_comp // 2
        sem = lambda *shape: [pltpu.SemaphoreType.DMA(shape), pltpu.SemaphoreType.DMA(shape)]
        vmem = pl.BlockSpec(memory_space=pltpu.VMEM)
        out = pl.pallas_call(
            functools.partial(kernel, n_dp, n_comp),
            out_shape=(
                jax.ShapeDtypeStruct((width, k_dev), F32),
                jax.ShapeDtypeStruct((width, k_dev), F32),
                jax.ShapeDtypeStruct((1, k_dev), F32),
            ),
            in_specs=[vmem] * 6,
            out_specs=(vmem, vmem, vmem),
            scratch_shapes=[
                pltpu.VMEM((npts, feats), BF),
                pltpu.VMEM((2, width, k_dev), BF),
                pltpu.VMEM((2, feats, chunk), BF),
                pltpu.VMEM((2, chunk, feats), BF),
                pltpu.VMEM((8, k_dev), F32),
                pltpu.VMEM((n_dp, 8, chunk), F32),
                pltpu.VMEM((n_dp, chunk, rows), F32),
                pltpu.VMEM((n_comp, n_dp, rows), F32),
                pltpu.VMEM((n_dp, n_dp, rows), F32),
                pltpu.VMEM((n_dp, rows), F32),
                pltpu.VMEM((chunk, npts), BF),
                pltpu.VMEM((2, feats, chunk), BF),
                pltpu.VMEM((2, width, k_dev), BF),
                pltpu.VMEM((8, chunk), F32),
                pltpu.VMEM((8, k_dev), F32),
                pltpu.VMEM((width, k_dev), F32),
                pltpu.VMEM((width, k_dev), F32),
                pltpu.VMEM((1, k_dev), F32),
                pltpu.VMEM((2, width + 8, spl), F32),
                pltpu.VMEM((n_comp, width + 16, 2 * spl), BF),
                *sem(far), *sem(far, near), *sem(n_dp, pairs), *sem(n_dp, pairs),
                *sem(n_dp), *sem(n_dp), *sem(n_comp), *sem(n_dp), *sem(n_dp), *sem(n_dp), *sem(n_comp),
            ],
            compiler_params=pltpu.CompilerParams(
                collective_id=0, has_side_effects=True, vmem_limit_bytes=56 * 1024 * 1024
            ),
        )(points, means, variances, log_weights[None, :], split_list, prune_list[None, :])
        return out[0], out[1], out[2][0]

    in_specs = (P("dp", None), P("dp", "comp"), P("dp", "comp"), P("comp"), P(), P())
    out_specs = (P("dp", "comp"), P("dp", "comp"), P("comp"))
    return jax.shard_map(per_device, mesh=mesh, in_specs=in_specs, out_specs=out_specs, check_vma=False)
```

```python
import functools
import math

import jax
import jax.numpy as jnp
from jax import lax
from jax.experimental import pallas as pl
from jax.experimental.pallas import tpu as pltpu
from jax.sharding import PartitionSpec as P

log_two_pi = math.log(2.0 * math.pi)
log_two = math.log(2.0)
prior_count = 1.0
split_scale = 0.5
MESH = pl.DeviceIdType.MESH
BF = jnp.bfloat16
F32 = jnp.float32
NT = (((1,), (1,)), ((), ()))


def aligned(index, step):
    return pl.ds(pl.multiple_of(index * step, step), step)


def kernel(
    n_dp, n_comp,
    pts, means, variances, weights, split, prune,
    out_mean, out_var, out_weight,
    allp, prm, par, par_t, cst_s, cst_r, scores, part_c, part_d, lse, resp,
    mom_s, mom_r, cnt_s, cnt_r, new_m, new_v, new_w, pay, got,
    z_s, z_r, y_s, y_r, x_s, x_r, c_s, c_r, p_s, p_r, k_s, k_r,
    lc_s, lc_r, ld_s, ld_r, m_s, m_r, n_s, n_r, g_s, g_r,
):
    rows, feats = pts.shape
    width, k_dev = means.shape
    chunk = k_dev // n_dp
    piece = rows // n_comp
    spl = split.shape[0] // n_comp
    far = 4 if n_dp % 4 == 0 else 1
    near = n_dp // far
    pairs = n_comp // 2
    i = lax.axis_index("dp")
    j = lax.axis_index("comp")
    a, b = i // near, i % near
    pair, core = j // 2, j % 2

    barrier = pltpu.get_barrier_semaphore()
    for r in range(1, n_dp):
        pl.semaphore_signal(barrier, inc=1, device_id=((i + r) % n_dp, j), device_id_type=MESH)
    for r in range(1, n_comp):
        pl.semaphore_signal(barrier, inc=1, device_id=(i, (j + r) % n_comp), device_id_type=MESH)
    pl.semaphore_wait(barrier, n_dp + n_comp - 2)

    def remote(src, dst, send, recv, to_i, to_j):
        return pltpu.make_async_remote_copy(
            src_ref=src, dst_ref=dst, send_sem=send, recv_sem=recv,
            device_id=(to_i, to_j), device_id_type=MESH,
        )

    inner = a * (3 - a) // 2
    upper = a // 2

    def plane(s):
        if far == 1:
            return a
        base = (s // 2) * s + (1 - s // 2) * (inner * (1 - s) + (1 - inner) * s)
        return base + upper * (3 - 2 * base)

    def block_of(s, t):
        return plane(s) * near + (b + near - t) % near

    def place(block, quarter):
        return allp.at[aligned(block * n_comp + quarter, piece), :]

    def own_piece():
        return pts.at[aligned(j, piece), :]

    def z_own(d):
        to = 3 * upper if d else 1 + a % 2
        return remote(own_piece(), place(i, j), z_s.at[a, d], z_r.at[a], to * near + b, j)

    def z_pass(s, to):
        src = place(block_of(s, 0), j)
        return remote(src, src, z_s.at[plane(s), 0], z_r.at[plane(s)], to * near + b, j)

    def z_in(s):
        return z_pass(s, (a + 1) % far)

    def z_on(s):
        return z_pass(s, 3 - a if s == 1 else 3 * upper)

    def y_copy(s, t):
        src = place(block_of(s, 0), j)
        return remote(src, src, y_s.at[s, t], y_r.at[s, t], a * near + (b + t) % near, j)

    def x_copy(idx, u):
        src = place(block_of(idx // near, idx % near), j)
        return remote(src, src, x_s.at[idx, u], x_r.at[idx, u], i, ((pair + u) % pairs) * 2 + core)

    def c_copy(idx, u):
        quarter = ((pair + pairs - u) % pairs) * 2 + core
        src = place(block_of(idx // near, idx % near), quarter)
        return remote(src, src, c_s.at[idx, u], c_r.at[idx, u], i, pair * 2 + 1 - core)

    if far > 1:
        z_own(0).start()

        @pl.when(inner == 1)
        def _():
            z_own(1).start()

    allp[aligned(i, rows), :] = pts[...]
    for t in range(1, near):
        y_copy(0, t).start()

    def make_params(to):
        cols = aligned(to, chunk)
        v = variances[:, cols]
        m = means[:, cols]
        p = 1.0 / v
        pm = p * m
        prm[0, :, cols] = p.astype(BF)
        prm[1, :, cols] = pm.astype(BF)
        part = -0.5 * jnp.sum(jnp.log(v) + pm * m, 0, keepdims=True)
        cst_s[:, cols] = jnp.broadcast_to(part, (8, chunk))

    def p_copy(r):
        to = (i + r) % n_dp
        return remote(prm.at[:, :, aligned(to, chunk)], par.at[:, aligned(i, width), :], p_s.at[r], p_r.at[r], to, j)

    def k_copy(r):
        to = (i + r) % n_dp
        return remote(cst_s.at[:, aligned(to, chunk)], cst_r.at[i], k_s.at[r], k_r.at[r], to, j)

    def send_params(r, carry):
        make_params((i + r) % n_dp)
        p_copy(r).start()
        k_copy(r).start()
        return carry

    lax.fori_loop(1, n_dp, send_params, 0)
    make_params(i)
    par[:, aligned(i, width), :] = prm[:, :, aligned(i, chunk)]
    cst_r[i] = cst_s[:, aligned(i, chunk)]

    def pass_on(idx):
        for u in range(1, pairs):
            x_copy(idx, u).start()
        c_copy(idx, 0).start()

    def pass_y(s):
        for t in range(1, near):
            y_copy(s, t).wait_recv()
            pass_on(s * near + t)

    for s in range(1, far):
        z_in(s).wait_recv()

        @pl.when(inner == 1)
        def _():
            z_on(s).start()

        for t in range(1, near):
            y_copy(s, t).start()
        pass_on(s * near)
        pass_y(s - 1)
    pass_y(far - 1)

    def wait_params(r, carry):
        p_copy(r).wait_recv()
        k_copy(r).wait_recv()
        return carry

    lax.fori_loop(1, n_dp, wait_params, 0)
    par_t[0] = (-0.5 * par[0].astype(F32)).T.astype(BF)
    par_t[1] = par[1].astype(F32).T.astype(BF)
    const_row = jnp.sum(cst_r[...], 0) + weights[:, aligned(i, chunk)] - 0.5 * feats * log_two_pi
    const = const_row.T[:, :1]

    def score(block):
        x = allp[aligned(block, rows), :]
        s = (
            lax.dot_general(par_t[0], x * x, NT, preferred_element_type=F32)
            + lax.dot_general(par_t[1], x, NT, preferred_element_type=F32)
            + const
        )
        scores[block] = s
        top = jnp.max(s, 0, keepdims=True)
        part_c[j, pl.ds(block, 1), :] = top + jnp.log(jnp.sum(jnp.exp(s - top), 0, keepdims=True))

    def pass_core(idx):
        for u in range(1, pairs):
            x_copy(idx, u).wait_recv()
            c_copy(idx, u).start()

    score(i)
    pass_core(1)

    def score_step(idx, carry):
        @pl.when(idx < n_dp - 1)
        def _():
            pass_core(idx + 1)

        for u in range(pairs):
            c_copy(idx, u).wait_recv()
        score(block_of(idx // near, idx % near))
        return carry

    lax.fori_loop(1, n_dp, score_step, 0)

    def joined(parts):
        top = jnp.max(parts, 0)
        return top + jnp.log(jnp.sum(jnp.exp(parts - top[None]), 0))

    def lc_copy(r):
        return remote(part_c.at[j], part_c.at[j], lc_s.at[r], lc_r.at[r], i, (j + r) % n_comp)

    def ld_copy(r):
        return remote(part_d.at[i], part_d.at[i], ld_s.at[r], ld_r.at[r], (i + r) % n_dp, j)

    for r in range(1, n_comp):
        lc_copy(r).start()
    for r in range(1, n_comp):
        lc_copy(r).wait_recv()
    part_d[i] = joined(part_c[...])
    for r in range(1, n_dp):
        ld_copy(r).start()
    for r in range(1, n_dp):
        ld_copy(r).wait_recv()
    lse[...] = joined(part_d[...])

    def respond(block, carry):
        value = jnp.exp(scores[block] - lse[pl.ds(block, 1), :]).astype(BF)
        resp[:, aligned(block, rows)] = value
        return carry + lax.dot_general(jnp.ones((8, rows), BF), value, NT, preferred_element_type=F32)

    cnt_s[...] = lax.fori_loop(0, n_dp, respond, jnp.zeros((8, chunk), F32))

    def n_copy(r):
        return remote(cnt_s, cnt_r.at[:, aligned(i, chunk)], n_s.at[r], n_r.at[r], (i + r) % n_dp, j)

    for r in range(1, n_dp):
        n_copy(r).start()
    cnt_r[:, aligned(i, chunk)] = cnt_s[...]

    def m_copy(r):
        to = (i + r) % n_dp
        return remote(
            mom_s.at[:, aligned(to, width), :], mom_r.at[:, :, aligned(i, chunk)], m_s.at[r], m_r.at[r], to, j
        )

    wide = max(width, 256)
    each = wide // width
    groups = feats // wide
    mine = i // each

    def moment(group):
        cols = aligned(group, wide)
        x = allp[:, cols]
        mom_s[0, cols, :] = jnp.dot(resp[...], x, preferred_element_type=F32).T.astype(BF)
        mom_s[1, cols, :] = jnp.dot(resp[...], x * x, preferred_element_type=F32).T.astype(BF)

    def moment_step(g, carry):
        group = (mine + g) % groups
        moment(group)
        for e in range(each):
            m_copy((group * each + e + n_dp - i) % n_dp).start()
        return carry

    lax.fori_loop(1, groups, moment_step, 0)
    moment(mine)
    for e in range(1, each):
        to = mine * each + (i % each + e) % each
        m_copy((to + n_dp - i) % n_dp).start()
    mom_r[:, :, aligned(i, chunk)] = mom_s[:, aligned(i, width), :]

    base = (j * k_dev).astype(F32)
    sources = split[aligned(j, spl), :][:, 0:1].astype(F32) - base
    n_total = math.log(n_dp * rows + n_comp * k_dev * prior_count)
    pay[...] = jnp.zeros_like(pay)

    def hot(ids, at):
        ids_at = lax.broadcasted_iota(jnp.int32, (ids.shape[0], chunk), 1) + at * chunk
        return ids == ids_at.astype(F32)

    def finish(at):
        cols = aligned(at, chunk)
        total = cnt_r[0:1, cols] + prior_count
        inverse = 1.0 / total
        old = means[:, cols]
        mean = (mom_r[0, :, cols].astype(F32) + prior_count * old) * inverse
        var = (mom_r[1, :, cols].astype(F32) + prior_count * (variances[:, cols] + old * old)) * inverse - mean * mean
        low = jnp.log(total) - n_total
        here = hot(sources, at)
        here_f = jnp.where(here, 1.0, 0.0)
        source = jnp.max(here_f, 0, keepdims=True)
        shift = jnp.where(source > 0.5, split_scale * jnp.sqrt(var), 0.0)
        low = low - log_two * source
        new_m[:, cols] = mean + shift
        new_v[:, cols] = var
        new_w[:, cols] = low
        low_high = low.astype(BF)
        low_rest = (low - low_high.astype(F32)).astype(BF)
        here_b = here_f.astype(BF)
        pay[0, :width, :] += lax.dot_general((mean - shift).astype(BF), here_b, NT, preferred_element_type=F32)
        pay[1, :width, :] += lax.dot_general(var.astype(BF), here_b, NT, preferred_element_type=F32)
        spread = lambda row: jnp.broadcast_to(row, (8, chunk))
        pay[0, width:, :] += lax.dot_general(spread(low_high), here_b, NT, preferred_element_type=F32)
        pay[1, width:, :] += lax.dot_general(spread(low_rest), here_b, NT, preferred_element_type=F32)

    finish(i)

    def finish_step(r, carry):
        n_copy(r).wait_recv()
        m_copy(r).wait_recv()
        finish((i + n_dp - r) % n_dp)
        return carry

    lax.fori_loop(1, n_dp, finish_step, 0)

    extra = 16
    got[j, :width, :] = jnp.concatenate([pay[0, :width, :], pay[1, :width, :]], 1).astype(BF)
    got[j, width : width + extra, :] = jnp.concatenate(
        [
            jnp.concatenate([pay[0, width:, :], pay[1, width:, :]], 1),
            jnp.ones((8, 2 * spl), F32),
        ],
        0,
    ).astype(BF)

    def g_copy(r):
        return remote(got.at[j], got.at[j], g_s.at[r], g_r.at[r], i, (j + r) % n_comp)

    for r in range(1, n_comp):
        g_copy(r).start()
    slots = split[:, 1:2]
    slot_at = lax.broadcasted_iota(jnp.int32, (split.shape[0], split.shape[0]), 1)
    targets = jnp.sum(jnp.where(slots == slot_at, prune[...].astype(F32), 0.0), 1, keepdims=True) - base
    blank = jnp.full((spl, 1), -1.0, F32)
    parts = [targets[q * spl : (q + 1) * spl] for q in range(n_comp)]
    left = jnp.concatenate([part for q in range(n_comp) for part in (parts[q], blank)], 0)
    right = jnp.concatenate([part for q in range(n_comp) for part in (blank, parts[q])], 0)
    for r in range(1, n_comp):
        g_copy(r).wait_recv()
    cat = jnp.concatenate([got[q] for q in range(n_comp)], 1)

    for at in range(n_dp):
        cols = pl.ds(at * chunk, chunk)
        hot_l = jnp.where(hot(left, at), 1.0, 0.0).astype(BF)
        hot_r = jnp.where(hot(right, at), 1.0, 0.0).astype(BF)
        got_m = jnp.dot(cat, hot_l, preferred_element_type=F32)
        got_v = jnp.dot(cat, hot_r, preferred_element_type=F32)
        takes = got_m[width + 8 : width + 9, :] > 0.5
        out_mean[:, cols] = jnp.where(takes, got_m[:width], new_m[:, cols])
        out_var[:, cols] = jnp.where(takes, got_v[:width], new_v[:, cols])
        moved = got_m[width : width + 1, :] + got_v[width : width + 1, :]
        out_weight[:, cols] = jnp.where(takes, moved, new_w[:, cols])

    if far > 1:
        z_own(0).wait_send()

        @pl.when(inner == 1)
        def _():
            z_own(1).wait_send()
            for s in range(1, far):
                z_on(s).wait_send()

    for s in range(far):
        for t in range(1, near):
            y_copy(s, t).wait_send()

    def drain(idx, carry):
        for u in range(1, pairs):
            x_copy(idx, u).wait_send()
        for u in range(pairs):
            c_copy(idx, u).wait_send()
        p_copy(idx).wait_send()
        k_copy(idx).wait_send()
        ld_copy(idx).wait_send()
        n_copy(idx).wait_send()
        m_copy(idx).wait_send()
        return carry

    lax.fori_loop(1, n_dp, drain, 0)
    for r in range(1, n_comp):
        lc_copy(r).wait_send()
        g_copy(r).wait_send()


def solution(mesh):
    n_dp, n_comp = mesh.shape["dp"], mesh.shape["comp"]

    def per_device(points, means, variances, log_weights, split_list, prune_list):
        rows, feats = points.shape
        width, k_dev = means.shape
        chunk = k_dev // n_dp
        npts = rows * n_dp
        spl = split_list.shape[0] // n_comp
        far = 4 if n_dp % 4 == 0 else 1
        near, pairs = n_dp // far, n_comp // 2
        sem = lambda *shape: [pltpu.SemaphoreType.DMA(shape), pltpu.SemaphoreType.DMA(shape)]
        vmem = pl.BlockSpec(memory_space=pltpu.VMEM)
        out = pl.pallas_call(
            functools.partial(kernel, n_dp, n_comp),
            out_shape=(
                jax.ShapeDtypeStruct((width, k_dev), F32),
                jax.ShapeDtypeStruct((width, k_dev), F32),
                jax.ShapeDtypeStruct((1, k_dev), F32),
            ),
            in_specs=[vmem] * 6,
            out_specs=(vmem, vmem, vmem),
            scratch_shapes=[
                pltpu.VMEM((npts, feats), BF),
                pltpu.VMEM((2, width, k_dev), BF),
                pltpu.VMEM((2, feats, chunk), BF),
                pltpu.VMEM((2, chunk, feats), BF),
                pltpu.VMEM((8, k_dev), F32),
                pltpu.VMEM((n_dp, 8, chunk), F32),
                pltpu.VMEM((n_dp, chunk, rows), F32),
                pltpu.VMEM((n_comp, n_dp, rows), F32),
                pltpu.VMEM((n_dp, n_dp, rows), F32),
                pltpu.VMEM((n_dp, rows), F32),
                pltpu.VMEM((chunk, npts), BF),
                pltpu.VMEM((2, feats, chunk), BF),
                pltpu.VMEM((2, width, k_dev), BF),
                pltpu.VMEM((8, chunk), F32),
                pltpu.VMEM((8, k_dev), F32),
                pltpu.VMEM((width, k_dev), F32),
                pltpu.VMEM((width, k_dev), F32),
                pltpu.VMEM((1, k_dev), F32),
                pltpu.VMEM((2, width + 8, spl), F32),
                pltpu.VMEM((n_comp, width + 16, 2 * spl), BF),
                pltpu.SemaphoreType.DMA((far, 2)), pltpu.SemaphoreType.DMA((far,)), *sem(far, near), *sem(n_dp, pairs), *sem(n_dp, pairs),
                *sem(n_dp), *sem(n_dp), *sem(n_comp), *sem(n_dp), *sem(n_dp), *sem(n_dp), *sem(n_comp),
            ],
            compiler_params=pltpu.CompilerParams(
                collective_id=0, has_side_effects=True, vmem_limit_bytes=56 * 1024 * 1024
            ),
        )(points, means, variances, log_weights[None, :], split_list, prune_list[None, :])
        return out[0], out[1], out[2][0]

    in_specs = (P("dp", None), P("dp", "comp"), P("dp", "comp"), P("comp"), P(), P())
    out_specs = (P("dp", "comp"), P("dp", "comp"), P("comp"))
    return jax.shard_map(per_device, mesh=mesh, in_specs=in_specs, out_specs=out_specs, check_vma=False)
```

```python
import functools
import math

import jax
import jax.numpy as jnp
from jax import lax
from jax.experimental import pallas as pl
from jax.experimental.pallas import tpu as pltpu
from jax.sharding import PartitionSpec as P

log_two_pi = math.log(2.0 * math.pi)
log_two = math.log(2.0)
prior_count = 1.0
split_scale = 0.5
MESH = pl.DeviceIdType.MESH
BF = jnp.bfloat16
F32 = jnp.float32
NT = (((1,), (1,)), ((), ()))


def aligned(index, step):
    return pl.ds(pl.multiple_of(index * step, step), step)


def kernel(
    n_dp, n_comp,
    pts, means, variances, weights, split, prune,
    out_mean, out_var, out_weight,
    allp, prm, par, par_t, cst_s, cst_r, scores, tops, part_c, part_d, lse, resp,
    mom_s, mom_r, cnt_s, cnt_r, new_m, new_v, new_w, pay, got, hots,
    z_s, z_r, y_s, y_r, x_s, x_r, c_s, c_r, p_s, p_r, k_s, k_r,
    lc_s, lc_r, ld_s, ld_r, m_s, m_r, n_s, n_r, g_s, g_r,
):
    rows, feats = pts.shape
    width, k_dev = means.shape
    chunk = k_dev // n_dp
    piece = rows // n_comp
    spl = split.shape[0] // n_comp
    far = 4 if n_dp % 4 == 0 else 1
    near = n_dp // far
    pairs = n_comp // 2
    i = lax.axis_index("dp")
    j = lax.axis_index("comp")
    a, b = i // near, i % near
    pair, core = j // 2, j % 2

    barrier = pltpu.get_barrier_semaphore()
    for r in range(1, n_dp):
        pl.semaphore_signal(barrier, inc=1, device_id=((i + r) % n_dp, j), device_id_type=MESH)
    for r in range(1, n_comp):
        pl.semaphore_signal(barrier, inc=1, device_id=(i, (j + r) % n_comp), device_id_type=MESH)
    pl.semaphore_wait(barrier, n_dp + n_comp - 2)

    def remote(src, dst, send, recv, to_i, to_j):
        return pltpu.make_async_remote_copy(
            src_ref=src, dst_ref=dst, send_sem=send, recv_sem=recv,
            device_id=(to_i, to_j), device_id_type=MESH,
        )

    inner = a * (3 - a) // 2
    upper = a // 2

    def plane(s):
        if far == 1:
            return a
        base = (s // 2) * s + (1 - s // 2) * (inner * (1 - s) + (1 - inner) * s)
        return base + upper * (3 - 2 * base)

    def block_of(s, t):
        return plane(s) * near + (b + near - t) % near

    def place(block, quarter):
        return allp.at[aligned(block * n_comp + quarter, piece), :]

    def own_piece():
        return pts.at[aligned(j, piece), :]

    def z_own(d):
        to = 3 * upper if d else 1 + a % 2
        return remote(own_piece(), place(i, j), z_s.at[a, d], z_r.at[a], to * near + b, j)

    def z_pass(s, to):
        src = place(block_of(s, 0), j)
        return remote(src, src, z_s.at[plane(s), 0], z_r.at[plane(s)], to * near + b, j)

    def z_in(s):
        return z_pass(s, (a + 1) % far)

    def z_on(s):
        return z_pass(s, 3 - a if s == 1 else 3 * upper)

    def y_copy(s, t):
        src = place(block_of(s, 0), j)
        return remote(src, src, y_s.at[s, t], y_r.at[s, t], a * near + (b + t) % near, j)

    def x_copy(idx, u):
        src = place(block_of(idx // near, idx % near), j)
        return remote(src, src, x_s.at[idx, u], x_r.at[idx, u], i, ((pair + u) % pairs) * 2 + core)

    def c_copy(idx, u):
        quarter = ((pair + pairs - u) % pairs) * 2 + core
        src = place(block_of(idx // near, idx % near), quarter)
        return remote(src, src, c_s.at[idx, u], c_r.at[idx, u], i, pair * 2 + 1 - core)

    if far > 1:
        z_own(0).start()

        @pl.when(inner == 1)
        def _():
            z_own(1).start()

    allp[aligned(i, rows), :] = pts[...]
    for t in range(1, near):
        y_copy(0, t).start()

    def make_params(to):
        cols = aligned(to, chunk)
        v = variances[:, cols]
        m = means[:, cols]
        p = 1.0 / v
        pm = p * m
        prm[0, :, cols] = p.astype(BF)
        prm[1, :, cols] = pm.astype(BF)
        part = -0.5 * jnp.sum(jnp.log(v) + pm * m, 0, keepdims=True)
        cst_s[:, cols] = jnp.broadcast_to(part, (8, chunk))

    def p_copy(r):
        to = (i + r) % n_dp
        return remote(prm.at[:, :, aligned(to, chunk)], par.at[:, aligned(i, width), :], p_s.at[r], p_r.at[r], to, j)

    def k_copy(r):
        to = (i + r) % n_dp
        return remote(cst_s.at[:, aligned(to, chunk)], cst_r.at[i], k_s.at[r], k_r.at[r], to, j)

    def send_params(r, carry):
        make_params((i + r) % n_dp)
        p_copy(r).start()
        k_copy(r).start()
        return carry

    lax.fori_loop(1, n_dp, send_params, 0)
    make_params(i)
    par[:, aligned(i, width), :] = prm[:, :, aligned(i, chunk)]
    cst_r[i] = cst_s[:, aligned(i, chunk)]

    def pass_on(idx):
        for u in range(1, pairs):
            x_copy(idx, u).start()
        c_copy(idx, 0).start()

    def pass_y(s):
        for t in range(1, near):
            y_copy(s, t).wait_recv()
            pass_on(s * near + t)

    for s in range(1, far):
        z_in(s).wait_recv()

        @pl.when(inner == 1)
        def _():
            z_on(s).start()

        for t in range(1, near):
            y_copy(s, t).start()
        pass_on(s * near)
        pass_y(s - 1)
    pass_y(far - 1)

    def wait_params(r, carry):
        p_copy(r).wait_recv()
        k_copy(r).wait_recv()
        return carry

    lax.fori_loop(1, n_dp, wait_params, 0)
    par_t[0] = (-0.5 * par[0].astype(F32)).T.astype(BF)
    par_t[1] = par[1].astype(F32).T.astype(BF)
    const_row = jnp.sum(cst_r[...], 0) + weights[:, aligned(i, chunk)] - 0.5 * feats * log_two_pi
    const = const_row.T[:, :1]

    def score(block):
        x = allp[aligned(block, rows), :]
        s = (
            lax.dot_general(par_t[0], x * x, NT, preferred_element_type=F32)
            + lax.dot_general(par_t[1], x, NT, preferred_element_type=F32)
            + const
        )
        top = jnp.max(s, 0, keepdims=True)
        e = jnp.exp(s - top)
        scores[block] = e
        tops[pl.ds(block, 1), :] = top
        part_c[j, pl.ds(block, 1), :] = top + jnp.log(jnp.sum(e, 0, keepdims=True))

    def pass_core(idx):
        for u in range(1, pairs):
            x_copy(idx, u).wait_recv()
            c_copy(idx, u).start()

    score(i)
    pass_core(1)

    def score_step(idx, carry):
        @pl.when(idx < n_dp - 1)
        def _():
            pass_core(idx + 1)

        for u in range(pairs):
            c_copy(idx, u).wait_recv()
        score(block_of(idx // near, idx % near))
        return carry

    lax.fori_loop(1, n_dp, score_step, 0)

    def joined(parts):
        top = jnp.max(parts, 0)
        return top + jnp.log(jnp.sum(jnp.exp(parts - top[None]), 0))

    def lc_copy(r):
        return remote(part_c.at[j], part_c.at[j], lc_s.at[r], lc_r.at[r], i, (j + r) % n_comp)

    def ld_copy(r):
        return remote(part_d.at[i], part_d.at[i], ld_s.at[r], ld_r.at[r], (i + r) % n_dp, j)

    for r in range(1, n_comp):
        lc_copy(r).start()
    for r in range(1, n_comp):
        lc_copy(r).wait_recv()
    part_d[i] = joined(part_c[...])
    for r in range(1, n_dp):
        ld_copy(r).start()
    for r in range(1, n_dp):
        ld_copy(r).wait_recv()
    lse[...] = jnp.exp(tops[...] - joined(part_d[...]))

    def respond(block, carry):
        value = (scores[block] * lse[pl.ds(block, 1), :]).astype(BF)
        resp[:, aligned(block, rows)] = value
        return carry + lax.dot_general(jnp.ones((8, rows), BF), value, NT, preferred_element_type=F32)

    cnt_s[...] = lax.fori_loop(0, n_dp, respond, jnp.zeros((8, chunk), F32))

    def n_copy(r):
        return remote(cnt_s, cnt_r.at[:, aligned(i, chunk)], n_s.at[r], n_r.at[r], (i + r) % n_dp, j)

    for r in range(1, n_dp):
        n_copy(r).start()
    cnt_r[:, aligned(i, chunk)] = cnt_s[...]

    def m_copy(r):
        to = (i + r) % n_dp
        return remote(
            mom_s.at[:, aligned(to, width), :], mom_r.at[:, :, aligned(i, chunk)], m_s.at[r], m_r.at[r], to, j
        )

    wide = max(width, 256)
    each = wide // width
    groups = feats // wide
    mine = i // each

    def moment(group):
        cols = aligned(group, wide)
        x = allp[:, cols]
        mom_s[0, cols, :] = jnp.dot(resp[...], x, preferred_element_type=F32).T.astype(BF)
        mom_s[1, cols, :] = jnp.dot(resp[...], x * x, preferred_element_type=F32).T.astype(BF)

    def moment_step(g, carry):
        group = (mine + g) % groups
        moment(group)
        for e in range(each):
            m_copy((group * each + e + n_dp - i) % n_dp).start()
        return carry

    lax.fori_loop(1, groups, moment_step, 0)
    moment(mine)
    for e in range(1, each):
        to = mine * each + (i % each + e) % each
        m_copy((to + n_dp - i) % n_dp).start()
    mom_r[:, :, aligned(i, chunk)] = mom_s[:, aligned(i, width), :]

    base = (j * k_dev).astype(F32)
    sources = split[aligned(j, spl), :][:, 0:1].astype(F32) - base
    n_total = math.log(n_dp * rows + n_comp * k_dev * prior_count)
    pay[...] = jnp.zeros_like(pay)

    def hot(ids, at):
        ids_at = lax.broadcasted_iota(jnp.int32, (ids.shape[0], chunk), 1) + at * chunk
        return ids == ids_at.astype(F32)

    def finish(at):
        cols = aligned(at, chunk)
        total = cnt_r[0:1, cols] + prior_count
        inverse = 1.0 / total
        old = means[:, cols]
        mean = (mom_r[0, :, cols].astype(F32) + prior_count * old) * inverse
        var = (mom_r[1, :, cols].astype(F32) + prior_count * (variances[:, cols] + old * old)) * inverse - mean * mean
        low = jnp.log(total) - n_total
        here = hot(sources, at)
        here_f = jnp.where(here, 1.0, 0.0)
        source = jnp.max(here_f, 0, keepdims=True)
        shift = jnp.where(source > 0.5, split_scale * jnp.sqrt(var), 0.0)
        low = low - log_two * source
        new_m[:, cols] = mean + shift
        new_v[:, cols] = var
        new_w[:, cols] = low
        low_high = low.astype(BF)
        low_rest = (low - low_high.astype(F32)).astype(BF)
        here_b = here_f.astype(BF)
        spread = lambda row: jnp.broadcast_to(row.astype(F32), (8, chunk))
        stack = jnp.concatenate([mean - shift, var, spread(low_high), spread(low_rest)], 0).astype(BF)
        pay[...] += lax.dot_general(stack, here_b, NT, preferred_element_type=F32)

    slots = split[:, 1:2]
    slot_at = lax.broadcasted_iota(jnp.int32, (split.shape[0], split.shape[0]), 1)
    targets = jnp.sum(jnp.where(slots == slot_at, prune[...].astype(F32), 0.0), 1, keepdims=True) - base

    def mark(at, carry):
        hots[:, aligned(at, chunk)] = jnp.where(hot(targets, at), 1.0, 0.0).astype(BF)
        return carry

    lax.fori_loop(0, n_dp, mark, 0)
    finish(i)

    def finish_step(r, carry):
        n_copy(r).wait_recv()
        m_copy(r).wait_recv()
        finish((i + n_dp - r) % n_dp)
        return carry

    lax.fori_loop(1, n_dp, finish_step, 0)

    extra = 16
    ends = 2 * width
    got[j, :width, :] = jnp.concatenate([pay[:width, :], pay[width:ends, :]], 1).astype(BF)
    got[j, width : width + extra, :] = jnp.concatenate(
        [
            jnp.concatenate([pay[ends : ends + 8, :], pay[ends + 8 :, :]], 1),
            jnp.ones((8, 2 * spl), F32),
        ],
        0,
    ).astype(BF)

    def g_copy(r):
        return remote(got.at[j], got.at[j], g_s.at[r], g_r.at[r], i, (j + r) % n_comp)

    for r in range(1, n_comp):
        g_copy(r).start()
    for r in range(1, n_comp):
        g_copy(r).wait_recv()
    whole = [got[q].astype(F32) for q in range(n_comp)]
    cat = jnp.concatenate(
        [
            jnp.concatenate([part[:, :spl] for part in whole], 1),
            jnp.concatenate([part[:, spl:] for part in whole], 1),
        ],
        0,
    ).astype(BF)
    half = width + extra

    for at in range(n_dp):
        cols = pl.ds(at * chunk, chunk)
        moved = jnp.dot(cat, hots[:, cols], preferred_element_type=F32)
        takes = moved[width + 8 : width + 9, :] > 0.5
        out_mean[:, cols] = jnp.where(takes, moved[:width], new_m[:, cols])
        out_var[:, cols] = jnp.where(takes, moved[half : half + width], new_v[:, cols])
        weight = moved[width : width + 1, :] + moved[half + width : half + width + 1, :]
        out_weight[:, cols] = jnp.where(takes, weight, new_w[:, cols])

    if far > 1:
        z_own(0).wait_send()

        @pl.when(inner == 1)
        def _():
            z_own(1).wait_send()
            for s in range(1, far):
                z_on(s).wait_send()

    for s in range(far):
        for t in range(1, near):
            y_copy(s, t).wait_send()

    def drain(idx, carry):
        for u in range(1, pairs):
            x_copy(idx, u).wait_send()
        for u in range(pairs):
            c_copy(idx, u).wait_send()
        p_copy(idx).wait_send()
        k_copy(idx).wait_send()
        ld_copy(idx).wait_send()
        n_copy(idx).wait_send()
        m_copy(idx).wait_send()
        return carry

    lax.fori_loop(1, n_dp, drain, 0)
    for r in range(1, n_comp):
        lc_copy(r).wait_send()
        g_copy(r).wait_send()


def solution(mesh):
    n_dp, n_comp = mesh.shape["dp"], mesh.shape["comp"]

    def per_device(points, means, variances, log_weights, split_list, prune_list):
        rows, feats = points.shape
        width, k_dev = means.shape
        chunk = k_dev // n_dp
        npts = rows * n_dp
        spl = split_list.shape[0] // n_comp
        far = 4 if n_dp % 4 == 0 else 1
        near, pairs = n_dp // far, n_comp // 2
        sem = lambda *shape: [pltpu.SemaphoreType.DMA(shape), pltpu.SemaphoreType.DMA(shape)]
        vmem = pl.BlockSpec(memory_space=pltpu.VMEM)
        out = pl.pallas_call(
            functools.partial(kernel, n_dp, n_comp),
            out_shape=(
                jax.ShapeDtypeStruct((width, k_dev), F32),
                jax.ShapeDtypeStruct((width, k_dev), F32),
                jax.ShapeDtypeStruct((1, k_dev), F32),
            ),
            in_specs=[vmem] * 6,
            out_specs=(vmem, vmem, vmem),
            scratch_shapes=[
                pltpu.VMEM((npts, feats), BF),
                pltpu.VMEM((2, width, k_dev), BF),
                pltpu.VMEM((2, feats, chunk), BF),
                pltpu.VMEM((2, chunk, feats), BF),
                pltpu.VMEM((8, k_dev), F32),
                pltpu.VMEM((n_dp, 8, chunk), F32),
                pltpu.VMEM((n_dp, chunk, rows), F32),
                pltpu.VMEM((n_dp, rows), F32),
                pltpu.VMEM((n_comp, n_dp, rows), F32),
                pltpu.VMEM((n_dp, n_dp, rows), F32),
                pltpu.VMEM((n_dp, rows), F32),
                pltpu.VMEM((chunk, npts), BF),
                pltpu.VMEM((2, feats, chunk), BF),
                pltpu.VMEM((2, width, k_dev), BF),
                pltpu.VMEM((8, chunk), F32),
                pltpu.VMEM((8, k_dev), F32),
                pltpu.VMEM((width, k_dev), F32),
                pltpu.VMEM((width, k_dev), F32),
                pltpu.VMEM((1, k_dev), F32),
                pltpu.VMEM((2 * width + 16, spl), F32),
                pltpu.VMEM((n_comp, width + 16, 2 * spl), BF),
                pltpu.VMEM((split_list.shape[0], k_dev), BF),
                pltpu.SemaphoreType.DMA((far, 2)), pltpu.SemaphoreType.DMA((far,)), *sem(far, near), *sem(n_dp, pairs), *sem(n_dp, pairs),
                *sem(n_dp), *sem(n_dp), *sem(n_comp), *sem(n_dp), *sem(n_dp), *sem(n_dp), *sem(n_comp),
            ],
            compiler_params=pltpu.CompilerParams(
                collective_id=0, has_side_effects=True, vmem_limit_bytes=56 * 1024 * 1024
            ),
        )(points, means, variances, log_weights[None, :], split_list, prune_list[None, :])
        return out[0], out[1], out[2][0]

    in_specs = (P("dp", None), P("dp", "comp"), P("dp", "comp"), P("comp"), P(), P())
    out_specs = (P("dp", "comp"), P("dp", "comp"), P("comp"))
    return jax.shard_map(per_device, mesh=mesh, in_specs=in_specs, out_specs=out_specs, check_vma=False)
```

```python
import functools
import math

import jax
import jax.numpy as jnp
from jax import lax
from jax.experimental import pallas as pl
from jax.experimental.pallas import tpu as pltpu
from jax.sharding import PartitionSpec as P

log_two_pi = math.log(2.0 * math.pi)
log_two = math.log(2.0)
prior_count = 1.0
split_scale = 0.5
MESH = pl.DeviceIdType.MESH
BF = jnp.bfloat16
F32 = jnp.float32
NT = (((1,), (1,)), ((), ()))


def aligned(index, step):
    return pl.ds(pl.multiple_of(index * step, step), step)


def kernel(
    n_dp, n_comp,
    pts, means, variances, weights, split, prune,
    out_mean, out_var, out_weight,
    allp, prm, par, par_t, cst_s, cst_r, scores, tops, part_c, part_d, lse, resp,
    mom_s, mom_r, cnt_s, cnt_r, new_m, new_v, new_w, pay, got, hots,
    z_s, z_r, y_s, y_r, x_s, x_r, c_s, c_r, p_s, p_r, k_s, k_r,
    lc_s, lc_r, ld_s, ld_r, m_s, m_r, n_s, n_r, g_s, g_r,
):
    rows, feats = pts.shape
    width, k_dev = means.shape
    chunk = k_dev // n_dp
    piece = rows // n_comp
    spl = split.shape[0] // n_comp
    far = 4 if n_dp % 4 == 0 else 1
    near = n_dp // far
    pairs = n_comp // 2
    i = lax.axis_index("dp")
    j = lax.axis_index("comp")
    a, b = i // near, i % near
    pair, core = j // 2, j % 2

    barrier = pltpu.get_barrier_semaphore()
    for r in range(1, n_dp):
        pl.semaphore_signal(barrier, inc=1, device_id=((i + r) % n_dp, j), device_id_type=MESH)
    for r in range(1, n_comp):
        pl.semaphore_signal(barrier, inc=1, device_id=(i, (j + r) % n_comp), device_id_type=MESH)
    pl.semaphore_wait(barrier, n_dp + n_comp - 2)

    def remote(src, dst, send, recv, to_i, to_j):
        return pltpu.make_async_remote_copy(
            src_ref=src, dst_ref=dst, send_sem=send, recv_sem=recv,
            device_id=(to_i, to_j), device_id_type=MESH,
        )

    inner = a * (3 - a) // 2
    upper = a // 2

    def plane(s):
        if far == 1:
            return a
        base = (s // 2) * s + (1 - s // 2) * (inner * (1 - s) + (1 - inner) * s)
        return base + upper * (3 - 2 * base)

    def block_of(s, t):
        return plane(s) * near + (b + near - t) % near

    def place(block, quarter):
        return allp.at[aligned(block * n_comp + quarter, piece), :]

    def own_piece():
        return pts.at[aligned(j, piece), :]

    def z_own(d):
        to = 3 * upper if d else 1 + a % 2
        return remote(own_piece(), place(i, j), z_s.at[a, d], z_r.at[a], to * near + b, j)

    def z_pass(s, to):
        src = place(block_of(s, 0), j)
        return remote(src, src, z_s.at[plane(s), 0], z_r.at[plane(s)], to * near + b, j)

    def z_in(s):
        return z_pass(s, (a + 1) % far)

    def z_on(s):
        return z_pass(s, 3 - a if s == 1 else 3 * upper)

    def y_copy(s, t):
        src = place(block_of(s, 0), j)
        return remote(src, src, y_s.at[s, t], y_r.at[s, t], a * near + (b + t) % near, j)

    def x_copy(idx, u):
        src = place(block_of(idx // near, idx % near), j)
        return remote(src, src, x_s.at[idx, u], x_r.at[idx, u], i, ((pair + u) % pairs) * 2 + core)

    def c_copy(idx, u):
        quarter = ((pair + pairs - u) % pairs) * 2 + core
        src = place(block_of(idx // near, idx % near), quarter)
        return remote(src, src, c_s.at[idx, u], c_r.at[idx, u], i, pair * 2 + 1 - core)

    if far > 1:
        z_own(0).start()

        @pl.when(inner == 1)
        def _():
            z_own(1).start()

    allp[aligned(i, rows), :] = pts[...]
    for t in range(1, near):
        y_copy(0, t).start()

    def make_params(to):
        cols = aligned(to, chunk)
        v = variances[:, cols]
        m = means[:, cols]
        p = 1.0 / v
        pm = p * m
        prm[0, :, cols] = p.astype(BF)
        prm[1, :, cols] = pm.astype(BF)
        part = -0.5 * jnp.sum(jnp.log(v) + pm * m, 0, keepdims=True)
        cst_s[:, cols] = jnp.broadcast_to(part, (8, chunk))

    def p_copy(r):
        to = (i + r) % n_dp
        return remote(prm.at[:, :, aligned(to, chunk)], par.at[:, aligned(i, width), :], p_s.at[r], p_r.at[r], to, j)

    def k_copy(r):
        to = (i + r) % n_dp
        return remote(cst_s.at[:, aligned(to, chunk)], cst_r.at[i], k_s.at[r], k_r.at[r], to, j)

    def each_params(r, carry):
        make_params((i + r) % n_dp)
        return carry

    def send_params(r, carry):
        p_copy(r).start()
        k_copy(r).start()
        return carry

    lax.fori_loop(0, n_dp, each_params, 0)
    par[:, aligned(i, width), :] = prm[:, :, aligned(i, chunk)]
    cst_r[i] = cst_s[:, aligned(i, chunk)]

    def pass_on(idx):
        for u in range(1, pairs):
            x_copy(idx, u).start()
        c_copy(idx, 0).start()

    def pass_y(s):
        for t in range(1, near):
            y_copy(s, t).wait_recv()
            pass_on(s * near + t)

    for s in range(1, far):
        z_in(s).wait_recv()

        @pl.when(inner == 1)
        def _():
            z_on(s).start()

        for t in range(1, near):
            y_copy(s, t).start()
        pass_on(s * near)
        pass_y(s - 1)
        if s == 1:
            lax.fori_loop(1, n_dp, send_params, 0)
    pass_y(far - 1)
    if far == 1:
        lax.fori_loop(1, n_dp, send_params, 0)

    def wait_params(r, carry):
        p_copy(r).wait_recv()
        k_copy(r).wait_recv()
        return carry

    lax.fori_loop(1, n_dp, wait_params, 0)
    par_t[0] = (-0.5 * par[0].astype(F32)).T.astype(BF)
    par_t[1] = par[1].astype(F32).T.astype(BF)
    const_row = jnp.sum(cst_r[...], 0) + weights[:, aligned(i, chunk)] - 0.5 * feats * log_two_pi
    const = const_row.T[:, :1]

    def score(block):
        x = allp[aligned(block, rows), :]
        s = (
            lax.dot_general(par_t[0], x * x, NT, preferred_element_type=F32)
            + lax.dot_general(par_t[1], x, NT, preferred_element_type=F32)
            + const
        )
        top = jnp.max(s, 0, keepdims=True)
        e = jnp.exp(s - top)
        scores[block] = e
        tops[pl.ds(block, 1), :] = top
        part_c[j, pl.ds(block, 1), :] = top + jnp.log(jnp.sum(e, 0, keepdims=True))

    def pass_core(idx):
        for u in range(1, pairs):
            x_copy(idx, u).wait_recv()
            c_copy(idx, u).start()

    score(i)
    pass_core(1)

    def score_step(idx, carry):
        @pl.when(idx < n_dp - 1)
        def _():
            pass_core(idx + 1)

        for u in range(pairs):
            c_copy(idx, u).wait_recv()
        score(block_of(idx // near, idx % near))
        return carry

    lax.fori_loop(1, n_dp, score_step, 0)

    def joined(parts):
        top = jnp.max(parts, 0)
        return top + jnp.log(jnp.sum(jnp.exp(parts - top[None]), 0))

    def lc_copy(r):
        return remote(part_c.at[j], part_c.at[j], lc_s.at[r], lc_r.at[r], i, (j + r) % n_comp)

    def ld_copy(r):
        return remote(part_d.at[i], part_d.at[i], ld_s.at[r], ld_r.at[r], (i + r) % n_dp, j)

    for r in range(1, n_comp):
        lc_copy(r).start()
    for r in range(1, n_comp):
        lc_copy(r).wait_recv()
    part_d[i] = joined(part_c[...])
    for r in range(1, n_dp):
        ld_copy(r).start()
    for r in range(1, n_dp):
        ld_copy(r).wait_recv()
    lse[...] = jnp.exp(tops[...] - joined(part_d[...]))

    def respond(block, carry):
        value = (scores[block] * lse[pl.ds(block, 1), :]).astype(BF)
        resp[:, aligned(block, rows)] = value
        return carry + lax.dot_general(jnp.ones((8, rows), BF), value, NT, preferred_element_type=F32)

    cnt_s[...] = lax.fori_loop(0, n_dp, respond, jnp.zeros((8, chunk), F32))

    def n_copy(r):
        return remote(cnt_s, cnt_r.at[:, aligned(i, chunk)], n_s.at[r], n_r.at[r], (i + r) % n_dp, j)

    for r in range(1, n_dp):
        n_copy(r).start()
    cnt_r[:, aligned(i, chunk)] = cnt_s[...]

    def m_copy(r):
        to = (i + r) % n_dp
        return remote(
            mom_s.at[:, aligned(to, width), :], mom_r.at[:, :, aligned(i, chunk)], m_s.at[r], m_r.at[r], to, j
        )

    wide = max(width, 256)
    each = wide // width
    groups = feats // wide
    mine = i // each

    def moment(group):
        cols = aligned(group, wide)
        x = allp[:, cols]
        mom_s[0, cols, :] = jnp.dot(resp[...], x, preferred_element_type=F32).T.astype(BF)
        mom_s[1, cols, :] = jnp.dot(resp[...], x * x, preferred_element_type=F32).T.astype(BF)

    def moment_step(g, carry):
        group = (mine + g) % groups
        moment(group)
        for e in range(each):
            m_copy((group * each + e + n_dp - i) % n_dp).start()
        return carry

    lax.fori_loop(1, groups, moment_step, 0)
    moment(mine)
    for e in range(1, each):
        to = mine * each + (i % each + e) % each
        m_copy((to + n_dp - i) % n_dp).start()
    mom_r[:, :, aligned(i, chunk)] = mom_s[:, aligned(i, width), :]

    base = (j * k_dev).astype(F32)
    sources = split[aligned(j, spl), :][:, 0:1].astype(F32) - base
    n_total = math.log(n_dp * rows + n_comp * k_dev * prior_count)
    pay[...] = jnp.zeros_like(pay)

    def hot(ids, at):
        ids_at = lax.broadcasted_iota(jnp.int32, (ids.shape[0], chunk), 1) + at * chunk
        return ids == ids_at.astype(F32)

    def finish(at):
        cols = aligned(at, chunk)
        total = cnt_r[0:1, cols] + prior_count
        inverse = 1.0 / total
        old = means[:, cols]
        mean = (mom_r[0, :, cols].astype(F32) + prior_count * old) * inverse
        var = (mom_r[1, :, cols].astype(F32) + prior_count * (variances[:, cols] + old * old)) * inverse - mean * mean
        low = jnp.log(total) - n_total
        here = hot(sources, at)
        here_f = jnp.where(here, 1.0, 0.0)
        source = jnp.max(here_f, 0, keepdims=True)
        shift = jnp.where(source > 0.5, split_scale * jnp.sqrt(var), 0.0)
        low = low - log_two * source
        new_m[:, cols] = mean + shift
        new_v[:, cols] = var
        new_w[:, cols] = low
        low_high = low.astype(BF)
        low_rest = (low - low_high.astype(F32)).astype(BF)
        here_b = here_f.astype(BF)
        spread = lambda row: jnp.broadcast_to(row.astype(F32), (8, chunk))
        stack = jnp.concatenate([mean - shift, var, spread(low_high), spread(low_rest)], 0).astype(BF)
        pay[...] += lax.dot_general(stack, here_b, NT, preferred_element_type=F32)

    slots = split[:, 1:2]
    slot_at = lax.broadcasted_iota(jnp.int32, (split.shape[0], split.shape[0]), 1)
    targets = jnp.sum(jnp.where(slots == slot_at, prune[...].astype(F32), 0.0), 1, keepdims=True) - base

    def mark(at, carry):
        hots[:, aligned(at, chunk)] = jnp.where(hot(targets, at), 1.0, 0.0).astype(BF)
        return carry

    lax.fori_loop(0, n_dp, mark, 0)
    finish(i)

    def finish_step(r, carry):
        n_copy(r).wait_recv()
        m_copy(r).wait_recv()
        finish((i + n_dp - r) % n_dp)
        return carry

    lax.fori_loop(1, n_dp, finish_step, 0)

    extra = 16
    ends = 2 * width
    got[j, :width, :] = jnp.concatenate([pay[:width, :], pay[width:ends, :]], 1).astype(BF)
    got[j, width : width + extra, :] = jnp.concatenate(
        [
            jnp.concatenate([pay[ends : ends + 8, :], pay[ends + 8 :, :]], 1),
            jnp.ones((8, 2 * spl), F32),
        ],
        0,
    ).astype(BF)

    def g_copy(r):
        return remote(got.at[j], got.at[j], g_s.at[r], g_r.at[r], i, (j + r) % n_comp)

    for r in range(1, n_comp):
        g_copy(r).start()
    for r in range(1, n_comp):
        g_copy(r).wait_recv()
    whole = [got[q].astype(F32) for q in range(n_comp)]
    cat = jnp.concatenate(
        [
            jnp.concatenate([part[:, :spl] for part in whole], 1),
            jnp.concatenate([part[:, spl:] for part in whole], 1),
        ],
        0,
    ).astype(BF)
    half = width + extra

    for at in range(n_dp):
        cols = pl.ds(at * chunk, chunk)
        moved = jnp.dot(cat, hots[:, cols], preferred_element_type=F32)
        takes = moved[width + 8 : width + 9, :] > 0.5
        out_mean[:, cols] = jnp.where(takes, moved[:width], new_m[:, cols])
        out_var[:, cols] = jnp.where(takes, moved[half : half + width], new_v[:, cols])
        weight = moved[width : width + 1, :] + moved[half + width : half + width + 1, :]
        out_weight[:, cols] = jnp.where(takes, weight, new_w[:, cols])

    if far > 1:
        z_own(0).wait_send()

        @pl.when(inner == 1)
        def _():
            z_own(1).wait_send()
            for s in range(1, far):
                z_on(s).wait_send()

    for s in range(far):
        for t in range(1, near):
            y_copy(s, t).wait_send()

    def drain(idx, carry):
        for u in range(1, pairs):
            x_copy(idx, u).wait_send()
        for u in range(pairs):
            c_copy(idx, u).wait_send()
        p_copy(idx).wait_send()
        k_copy(idx).wait_send()
        ld_copy(idx).wait_send()
        n_copy(idx).wait_send()
        m_copy(idx).wait_send()
        return carry

    lax.fori_loop(1, n_dp, drain, 0)
    for r in range(1, n_comp):
        lc_copy(r).wait_send()
        g_copy(r).wait_send()


def solution(mesh):
    n_dp, n_comp = mesh.shape["dp"], mesh.shape["comp"]

    def per_device(points, means, variances, log_weights, split_list, prune_list):
        rows, feats = points.shape
        width, k_dev = means.shape
        chunk = k_dev // n_dp
        npts = rows * n_dp
        spl = split_list.shape[0] // n_comp
        far = 4 if n_dp % 4 == 0 else 1
        near, pairs = n_dp // far, n_comp // 2
        sem = lambda *shape: [pltpu.SemaphoreType.DMA(shape), pltpu.SemaphoreType.DMA(shape)]
        vmem = pl.BlockSpec(memory_space=pltpu.VMEM)
        out = pl.pallas_call(
            functools.partial(kernel, n_dp, n_comp),
            out_shape=(
                jax.ShapeDtypeStruct((width, k_dev), F32),
                jax.ShapeDtypeStruct((width, k_dev), F32),
                jax.ShapeDtypeStruct((1, k_dev), F32),
            ),
            in_specs=[vmem] * 6,
            out_specs=(vmem, vmem, vmem),
            scratch_shapes=[
                pltpu.VMEM((npts, feats), BF),
                pltpu.VMEM((2, width, k_dev), BF),
                pltpu.VMEM((2, feats, chunk), BF),
                pltpu.VMEM((2, chunk, feats), BF),
                pltpu.VMEM((8, k_dev), F32),
                pltpu.VMEM((n_dp, 8, chunk), F32),
                pltpu.VMEM((n_dp, chunk, rows), F32),
                pltpu.VMEM((n_dp, rows), F32),
                pltpu.VMEM((n_comp, n_dp, rows), F32),
                pltpu.VMEM((n_dp, n_dp, rows), F32),
                pltpu.VMEM((n_dp, rows), F32),
                pltpu.VMEM((chunk, npts), BF),
                pltpu.VMEM((2, feats, chunk), BF),
                pltpu.VMEM((2, width, k_dev), BF),
                pltpu.VMEM((8, chunk), F32),
                pltpu.VMEM((8, k_dev), F32),
                pltpu.VMEM((width, k_dev), F32),
                pltpu.VMEM((width, k_dev), F32),
                pltpu.VMEM((1, k_dev), F32),
                pltpu.VMEM((2 * width + 16, spl), F32),
                pltpu.VMEM((n_comp, width + 16, 2 * spl), BF),
                pltpu.VMEM((split_list.shape[0], k_dev), BF),
                pltpu.SemaphoreType.DMA((far, 2)), pltpu.SemaphoreType.DMA((far,)), *sem(far, near), *sem(n_dp, pairs), *sem(n_dp, pairs),
                *sem(n_dp), *sem(n_dp), *sem(n_comp), *sem(n_dp), *sem(n_dp), *sem(n_dp), *sem(n_comp),
            ],
            compiler_params=pltpu.CompilerParams(
                collective_id=0, has_side_effects=True, vmem_limit_bytes=56 * 1024 * 1024
            ),
        )(points, means, variances, log_weights[None, :], split_list, prune_list[None, :])
        return out[0], out[1], out[2][0]

    in_specs = (P("dp", None), P("dp", "comp"), P("dp", "comp"), P("comp"), P(), P())
    out_specs = (P("dp", "comp"), P("dp", "comp"), P("comp"))
    return jax.shard_map(per_device, mesh=mesh, in_specs=in_specs, out_specs=out_specs, check_vma=False)
```

```python
import functools
import math

import jax
import jax.numpy as jnp
from jax import lax
from jax.experimental import pallas as pl
from jax.experimental.pallas import tpu as pltpu
from jax.sharding import PartitionSpec as P

log_two_pi = math.log(2.0 * math.pi)
log_two = math.log(2.0)
prior_count = 1.0
split_scale = 0.5
MESH = pl.DeviceIdType.MESH
BF = jnp.bfloat16
F32 = jnp.float32
NT = (((1,), (1,)), ((), ()))


def aligned(index, step):
    return pl.ds(pl.multiple_of(index * step, step), step)


def kernel(
    n_dp, n_comp,
    pts, means, variances, weights, split, prune,
    out_mean, out_var, out_weight,
    allp, prm, par, par_t, cst_s, cst_r, scores, tops, part_c, part_d, lse, resp,
    mom_s, mom_r, cnt_s, cnt_r, new_m, new_v, new_w, pay, got, hots,
    z_s, z_r, y_s, y_r, x_s, x_r, c_s, c_r, p_s, p_r, k_s, k_r,
    lc_s, lc_r, ld_s, ld_r, m_s, m_r, n_s, n_r, g_s, g_r,
):
    rows, feats = pts.shape
    width, k_dev = means.shape
    chunk = k_dev // n_dp
    piece = rows // n_comp
    spl = split.shape[0] // n_comp
    far = 4 if n_dp % 4 == 0 else 1
    near = n_dp // far
    pairs = n_comp // 2
    i = lax.axis_index("dp")
    j = lax.axis_index("comp")
    a, b = i // near, i % near
    pair, core = j // 2, j % 2

    barrier = pltpu.get_barrier_semaphore()
    for r in range(1, n_dp):
        pl.semaphore_signal(barrier, inc=1, device_id=((i + r) % n_dp, j), device_id_type=MESH)
    for r in range(1, n_comp):
        pl.semaphore_signal(barrier, inc=1, device_id=(i, (j + r) % n_comp), device_id_type=MESH)
    pl.semaphore_wait(barrier, n_dp + n_comp - 2)

    def remote(src, dst, send, recv, to_i, to_j):
        return pltpu.make_async_remote_copy(
            src_ref=src, dst_ref=dst, send_sem=send, recv_sem=recv,
            device_id=(to_i, to_j), device_id_type=MESH,
        )

    inner = a * (3 - a) // 2
    upper = a // 2

    def plane(s):
        if far == 1:
            return a
        base = (s // 2) * s + (1 - s // 2) * (inner * (1 - s) + (1 - inner) * s)
        return base + upper * (3 - 2 * base)

    def block_of(s, t):
        return plane(s) * near + (b + near - t) % near

    def place(block, quarter):
        return allp.at[aligned(block * n_comp + quarter, piece), :]

    def own_piece():
        return pts.at[aligned(j, piece), :]

    def z_own(d):
        to = 3 * upper if d else 1 + a % 2
        return remote(own_piece(), place(i, j), z_s.at[a, d], z_r.at[a], to * near + b, j)

    def z_pass(s, to):
        src = place(block_of(s, 0), j)
        return remote(src, src, z_s.at[plane(s), 0], z_r.at[plane(s)], to * near + b, j)

    def z_in(s):
        return z_pass(s, (a + 1) % far)

    def z_on(s):
        return z_pass(s, 3 - a if s == 1 else 3 * upper)

    def y_copy(s, t):
        src = place(block_of(s, 0), j)
        return remote(src, src, y_s.at[s, t], y_r.at[s, t], a * near + (b + t) % near, j)

    def x_copy(idx, u):
        src = place(block_of(idx // near, idx % near), j)
        return remote(src, src, x_s.at[idx, u], x_r.at[idx, u], i, ((pair + u) % pairs) * 2 + core)

    def yx_copy(t, u):
        src = place(i, ((pair + pairs - u) % pairs) * 2 + core)
        return remote(src, src, x_s.at[t, u], x_r.at[t, u], a * near + (b + t) % near, j)

    def c_copy(idx, u):
        quarter = ((pair + pairs - u) % pairs) * 2 + core
        src = place(block_of(idx // near, idx % near), quarter)
        return remote(src, src, c_s.at[idx, u], c_r.at[idx, u], i, pair * 2 + 1 - core)

    if far > 1:
        z_own(0).start()

        @pl.when(inner == 1)
        def _():
            z_own(1).start()

    allp[aligned(i, rows), :] = pts[...]
    for t in range(1, near):
        y_copy(0, t).start()
        for u in range(1, pairs):
            yx_copy(t, u).start()

    def make_params(to):
        cols = aligned(to, chunk)
        v = variances[:, cols]
        m = means[:, cols]
        p = 1.0 / v
        pm = p * m
        prm[0, :, cols] = p.astype(BF)
        prm[1, :, cols] = pm.astype(BF)
        part = -0.5 * jnp.sum(jnp.log(v) + pm * m, 0, keepdims=True)
        cst_s[:, cols] = jnp.broadcast_to(part, (8, chunk))

    def p_copy(r):
        to = (i + r) % n_dp
        return remote(prm.at[:, :, aligned(to, chunk)], par.at[:, aligned(i, width), :], p_s.at[r], p_r.at[r], to, j)

    def k_copy(r):
        to = (i + r) % n_dp
        return remote(cst_s.at[:, aligned(to, chunk)], cst_r.at[i], k_s.at[r], k_r.at[r], to, j)

    def each_params(r, carry):
        make_params((i + r) % n_dp)
        return carry

    def send_params(r, carry):
        p_copy(r).start()
        k_copy(r).start()
        return carry

    lax.fori_loop(0, n_dp, each_params, 0)
    par[:, aligned(i, width), :] = prm[:, :, aligned(i, chunk)]
    cst_r[i] = cst_s[:, aligned(i, chunk)]

    def pass_on(idx):
        if idx >= near:
            for u in range(1, pairs):
                x_copy(idx, u).start()
        c_copy(idx, 0).start()

    def pass_y(s):
        for t in range(1, near):
            y_copy(s, t).wait_recv()
            pass_on(s * near + t)

    for s in range(1, far):
        z_in(s).wait_recv()

        @pl.when(inner == 1)
        def _():
            z_on(s).start()

        for t in range(1, near):
            y_copy(s, t).start()
        pass_on(s * near)
        pass_y(s - 1)
        if s == 1:
            lax.fori_loop(1, n_dp, send_params, 0)
    pass_y(far - 1)
    if far == 1:
        lax.fori_loop(1, n_dp, send_params, 0)

    def wait_params(r, carry):
        p_copy(r).wait_recv()
        k_copy(r).wait_recv()
        return carry

    lax.fori_loop(1, n_dp, wait_params, 0)
    par_t[0] = (-0.5 * par[0].astype(F32)).T.astype(BF)
    par_t[1] = par[1].astype(F32).T.astype(BF)
    const_row = jnp.sum(cst_r[...], 0) + weights[:, aligned(i, chunk)] - 0.5 * feats * log_two_pi
    const = const_row.T[:, :1]

    def score(block):
        x = allp[aligned(block, rows), :]
        s = (
            lax.dot_general(par_t[0], x * x, NT, preferred_element_type=F32)
            + lax.dot_general(par_t[1], x, NT, preferred_element_type=F32)
            + const
        )
        top = jnp.max(s, 0, keepdims=True)
        e = jnp.exp(s - top)
        scores[block] = e
        tops[pl.ds(block, 1), :] = top
        part_c[j, pl.ds(block, 1), :] = top + jnp.log(jnp.sum(e, 0, keepdims=True))

    def pass_core(idx):
        for u in range(1, pairs):
            x_copy(idx, u).wait_recv()
            c_copy(idx, u).start()

    score(i)
    pass_core(1)

    def score_step(idx, carry):
        @pl.when(idx < n_dp - 1)
        def _():
            pass_core(idx + 1)

        for u in range(pairs):
            c_copy(idx, u).wait_recv()
        score(block_of(idx // near, idx % near))
        return carry

    lax.fori_loop(1, n_dp, score_step, 0)

    def joined(parts):
        top = jnp.max(parts, 0)
        return top + jnp.log(jnp.sum(jnp.exp(parts - top[None]), 0))

    def lc_copy(r):
        return remote(part_c.at[j], part_c.at[j], lc_s.at[r], lc_r.at[r], i, (j + r) % n_comp)

    def ld_copy(r):
        return remote(part_d.at[i], part_d.at[i], ld_s.at[r], ld_r.at[r], (i + r) % n_dp, j)

    for r in range(1, n_comp):
        lc_copy(r).start()
    for r in range(1, n_comp):
        lc_copy(r).wait_recv()
    part_d[i] = joined(part_c[...])
    for r in range(1, n_dp):
        ld_copy(r).start()
    for r in range(1, n_dp):
        ld_copy(r).wait_recv()
    lse[...] = jnp.exp(tops[...] - joined(part_d[...]))

    def respond(block, carry):
        value = (scores[block] * lse[pl.ds(block, 1), :]).astype(BF)
        resp[:, aligned(block, rows)] = value
        return carry + lax.dot_general(jnp.ones((8, rows), BF), value, NT, preferred_element_type=F32)

    cnt_s[...] = lax.fori_loop(0, n_dp, respond, jnp.zeros((8, chunk), F32))

    def n_copy(r):
        return remote(cnt_s, cnt_r.at[:, aligned(i, chunk)], n_s.at[r], n_r.at[r], (i + r) % n_dp, j)

    for r in range(1, n_dp):
        n_copy(r).start()
    cnt_r[:, aligned(i, chunk)] = cnt_s[...]

    def m_copy(r):
        to = (i + r) % n_dp
        return remote(
            mom_s.at[:, aligned(to, width), :], mom_r.at[:, :, aligned(i, chunk)], m_s.at[r], m_r.at[r], to, j
        )

    wide = max(width, 256)
    each = wide // width
    groups = feats // wide
    mine = i // each

    def moment(group):
        cols = aligned(group, wide)
        x = allp[:, cols]
        mom_s[0, cols, :] = jnp.dot(resp[...], x, preferred_element_type=F32).T.astype(BF)
        mom_s[1, cols, :] = jnp.dot(resp[...], x * x, preferred_element_type=F32).T.astype(BF)

    def moment_step(g, carry):
        group = (mine + g) % groups
        moment(group)
        for e in range(each):
            m_copy((group * each + e + n_dp - i) % n_dp).start()
        return carry

    lax.fori_loop(1, groups, moment_step, 0)
    moment(mine)
    for e in range(1, each):
        to = mine * each + (i % each + e) % each
        m_copy((to + n_dp - i) % n_dp).start()
    mom_r[:, :, aligned(i, chunk)] = mom_s[:, aligned(i, width), :]

    base = (j * k_dev).astype(F32)
    sources = split[aligned(j, spl), :][:, 0:1].astype(F32) - base
    n_total = math.log(n_dp * rows + n_comp * k_dev * prior_count)
    pay[...] = jnp.zeros_like(pay)

    def hot(ids, at):
        ids_at = lax.broadcasted_iota(jnp.int32, (ids.shape[0], chunk), 1) + at * chunk
        return ids == ids_at.astype(F32)

    def finish(at):
        cols = aligned(at, chunk)
        total = cnt_r[0:1, cols] + prior_count
        inverse = 1.0 / total
        old = means[:, cols]
        mean = (mom_r[0, :, cols].astype(F32) + prior_count * old) * inverse
        var = (mom_r[1, :, cols].astype(F32) + prior_count * (variances[:, cols] + old * old)) * inverse - mean * mean
        low = jnp.log(total) - n_total
        here = hot(sources, at)
        here_f = jnp.where(here, 1.0, 0.0)
        source = jnp.max(here_f, 0, keepdims=True)
        shift = jnp.where(source > 0.5, split_scale * jnp.sqrt(var), 0.0)
        low = low - log_two * source
        new_m[:, cols] = mean + shift
        new_v[:, cols] = var
        new_w[:, cols] = low
        low_high = low.astype(BF)
        low_rest = (low - low_high.astype(F32)).astype(BF)
        here_b = here_f.astype(BF)
        spread = lambda row: jnp.broadcast_to(row.astype(F32), (8, chunk))
        stack = jnp.concatenate([mean - shift, var, spread(low_high), spread(low_rest)], 0).astype(BF)
        pay[...] += lax.dot_general(stack, here_b, NT, preferred_element_type=F32)

    slots = split[:, 1:2]
    slot_at = lax.broadcasted_iota(jnp.int32, (split.shape[0], split.shape[0]), 1)
    targets = jnp.sum(jnp.where(slots == slot_at, prune[...].astype(F32), 0.0), 1, keepdims=True) - base

    def mark(at, carry):
        hots[:, aligned(at, chunk)] = jnp.where(hot(targets, at), 1.0, 0.0).astype(BF)
        return carry

    lax.fori_loop(0, n_dp, mark, 0)
    finish(i)

    def finish_step(r, carry):
        n_copy(r).wait_recv()
        m_copy(r).wait_recv()
        finish((i + n_dp - r) % n_dp)
        return carry

    lax.fori_loop(1, n_dp, finish_step, 0)

    extra = 16
    ends = 2 * width
    got[j, :width, :] = jnp.concatenate([pay[:width, :], pay[width:ends, :]], 1).astype(BF)
    got[j, width : width + extra, :] = jnp.concatenate(
        [
            jnp.concatenate([pay[ends : ends + 8, :], pay[ends + 8 :, :]], 1),
            jnp.ones((8, 2 * spl), F32),
        ],
        0,
    ).astype(BF)

    def g_copy(r):
        return remote(got.at[j], got.at[j], g_s.at[r], g_r.at[r], i, (j + r) % n_comp)

    for r in range(1, n_comp):
        g_copy(r).start()
    for r in range(1, n_comp):
        g_copy(r).wait_recv()
    whole = [got[q].astype(F32) for q in range(n_comp)]
    cat = jnp.concatenate(
        [
            jnp.concatenate([part[:, :spl] for part in whole], 1),
            jnp.concatenate([part[:, spl:] for part in whole], 1),
        ],
        0,
    ).astype(BF)
    half = width + extra

    for at in range(n_dp):
        cols = pl.ds(at * chunk, chunk)
        moved = jnp.dot(cat, hots[:, cols], preferred_element_type=F32)
        takes = moved[width + 8 : width + 9, :] > 0.5
        out_mean[:, cols] = jnp.where(takes, moved[:width], new_m[:, cols])
        out_var[:, cols] = jnp.where(takes, moved[half : half + width], new_v[:, cols])
        weight = moved[width : width + 1, :] + moved[half + width : half + width + 1, :]
        out_weight[:, cols] = jnp.where(takes, weight, new_w[:, cols])

    if far > 1:
        z_own(0).wait_send()

        @pl.when(inner == 1)
        def _():
            z_own(1).wait_send()
            for s in range(1, far):
                z_on(s).wait_send()

    for s in range(far):
        for t in range(1, near):
            y_copy(s, t).wait_send()

    def drain(idx, carry):
        for u in range(1, pairs):
            x_copy(idx, u).wait_send()
        for u in range(pairs):
            c_copy(idx, u).wait_send()
        p_copy(idx).wait_send()
        k_copy(idx).wait_send()
        ld_copy(idx).wait_send()
        n_copy(idx).wait_send()
        m_copy(idx).wait_send()
        return carry

    lax.fori_loop(1, n_dp, drain, 0)
    for r in range(1, n_comp):
        lc_copy(r).wait_send()
        g_copy(r).wait_send()


def solution(mesh):
    n_dp, n_comp = mesh.shape["dp"], mesh.shape["comp"]

    def per_device(points, means, variances, log_weights, split_list, prune_list):
        rows, feats = points.shape
        width, k_dev = means.shape
        chunk = k_dev // n_dp
        npts = rows * n_dp
        spl = split_list.shape[0] // n_comp
        far = 4 if n_dp % 4 == 0 else 1
        near, pairs = n_dp // far, n_comp // 2
        sem = lambda *shape: [pltpu.SemaphoreType.DMA(shape), pltpu.SemaphoreType.DMA(shape)]
        vmem = pl.BlockSpec(memory_space=pltpu.VMEM)
        out = pl.pallas_call(
            functools.partial(kernel, n_dp, n_comp),
            out_shape=(
                jax.ShapeDtypeStruct((width, k_dev), F32),
                jax.ShapeDtypeStruct((width, k_dev), F32),
                jax.ShapeDtypeStruct((1, k_dev), F32),
            ),
            in_specs=[vmem] * 6,
            out_specs=(vmem, vmem, vmem),
            scratch_shapes=[
                pltpu.VMEM((npts, feats), BF),
                pltpu.VMEM((2, width, k_dev), BF),
                pltpu.VMEM((2, feats, chunk), BF),
                pltpu.VMEM((2, chunk, feats), BF),
                pltpu.VMEM((8, k_dev), F32),
                pltpu.VMEM((n_dp, 8, chunk), F32),
                pltpu.VMEM((n_dp, chunk, rows), F32),
                pltpu.VMEM((n_dp, rows), F32),
                pltpu.VMEM((n_comp, n_dp, rows), F32),
                pltpu.VMEM((n_dp, n_dp, rows), F32),
                pltpu.VMEM((n_dp, rows), F32),
                pltpu.VMEM((chunk, npts), BF),
                pltpu.VMEM((2, feats, chunk), BF),
                pltpu.VMEM((2, width, k_dev), BF),
                pltpu.VMEM((8, chunk), F32),
                pltpu.VMEM((8, k_dev), F32),
                pltpu.VMEM((width, k_dev), F32),
                pltpu.VMEM((width, k_dev), F32),
                pltpu.VMEM((1, k_dev), F32),
                pltpu.VMEM((2 * width + 16, spl), F32),
                pltpu.VMEM((n_comp, width + 16, 2 * spl), BF),
                pltpu.VMEM((split_list.shape[0], k_dev), BF),
                pltpu.SemaphoreType.DMA((far, 2)), pltpu.SemaphoreType.DMA((far,)), *sem(far, near), *sem(n_dp, pairs), *sem(n_dp, pairs),
                *sem(n_dp), *sem(n_dp), *sem(n_comp), *sem(n_dp), *sem(n_dp), *sem(n_dp), *sem(n_comp),
            ],
            compiler_params=pltpu.CompilerParams(
                collective_id=0, has_side_effects=True, vmem_limit_bytes=56 * 1024 * 1024
            ),
        )(points, means, variances, log_weights[None, :], split_list, prune_list[None, :])
        return out[0], out[1], out[2][0]

    in_specs = (P("dp", None), P("dp", "comp"), P("dp", "comp"), P("comp"), P(), P())
    out_specs = (P("dp", "comp"), P("dp", "comp"), P("comp"))
    return jax.shard_map(per_device, mesh=mesh, in_specs=in_specs, out_specs=out_specs, check_vma=False)
```
